32 devices in a mesh: ctx: 16 (over z, y, core), head: 2 (over x).
Axes of the slice: x: 2, y: 2, z: 4, core: 2. Of those that a mesh axis runs over, the one named last changes fastest.
Arguments:
- events: bfloat16 [4096, 1024], P('ctx'), may hold values from -8 to 8
- ssm_input: bfloat16 [4096, 2048], P('ctx', 'head'), may hold values from -1.5 to 1.5
- gate_input: bfloat16 [4096, 2048], P('ctx', 'head'), may hold values from -6 to 6
- grad_out: bfloat16 [4096, 2048], P('ctx', 'head'), may hold values from -0.015625 to 0.015625
- shared_b: bfloat16 [4096, 128], P('ctx'), may hold values from -6 to 6
- shared_c: bfloat16 [4096, 128], P('ctx'), may hold values from -6 to 6
- log_decay: float32 [32, 4096], P('head', 'ctx'), may hold values from -1 to 0, as said below
- entry_state: float32 [16, 32, 128, 64], P('ctx', 'head'), may hold values from -48 to 48
- w_gate: bfloat16 [1024, 2048], P(None, 'head'), may hold values from -0.1875 to 0.1875
- w_value: bfloat16 [1024, 2048], P(None, 'head'), may hold values from -0.1875 to 0.1875
- w_shared: bfloat16 [1024, 256], P(None, 'head'), may hold values from -0.1875 to 0.1875
Outputs:
- grad_input: bfloat16 [4096, 1024], P('ctx', 'head')
- grad_w_gate: float32 [1024, 2048], P('ctx', 'head')
- grad_w_value: float32 [1024, 2048], P('ctx', 'head')
- grad_w_shared: float32 [1024, 256], P('ctx', 'head')
The draws below stay inside these ranges and needn't reach their ends.
Inputs may be any that keep to these rules, and one draw needn't show every extreme that they name: `log_decay`: every entry is negative.
All inputs are finite; a program needn't handle non-finite values.
Results may differ from the reference program's by a relative error of at most 0.015.
Values may be sent and summed in bfloat16 or wider, within the bound.
A program may use at most 64 MiB of HBM per device.

```python
import math
import jax
import jax.numpy as jnp
from jax import lax

D = 1024
HEAD_TOTAL = 32
HEAD_DIM = 64
STATE = 128
SPAN = 256
L_DEV = 256
TOKEN_COUNT = 4096
BLOCKS = 16
GROUP_HEADS = 16
N_HEAD = 2


def draw_log_decay(key, part):
    random_subkeys = jax.random.split(key, 7)
    fast_share = 5
    fast_heads = jax.random.randint(random_subkeys[0], (HEAD_TOTAL,), 0, 10) < fast_share
    fast_rates = jnp.exp(jax.random.uniform(random_subkeys[1], (HEAD_TOTAL,), jnp.float32, math.log(1.0 / 50.0), math.log(1.0 / 30.0)))
    slow_rates = 0.12 * math.log(10.0) / TOKEN_COUNT * jax.random.uniform(random_subkeys[2], (HEAD_TOTAL,), jnp.float32, 0.5, 1.0)
    head_rates = jnp.where(fast_heads, fast_rates, slow_rates)
    blocks = TOKEN_COUNT // L_DEV
    block_factor = jnp.exp(jax.random.uniform(random_subkeys[3], (HEAD_TOTAL, blocks, 1), jnp.float32, math.log(0.5), math.log(2.0)))
    event_factor = jax.random.uniform(random_subkeys[4], (HEAD_TOTAL, blocks, L_DEV), jnp.float32, 0.5, 1.5)
    forget_rates = -(head_rates[:, None, None] * block_factor * event_factor).reshape(HEAD_TOTAL, TOKEN_COUNT)
    spike_position = jax.random.randint(random_subkeys[5], (HEAD_TOTAL, 2), 0, TOKEN_COUNT)
    spike_penalty = jax.random.uniform(random_subkeys[6], (HEAD_TOTAL, 2), jnp.float32, math.log(0.5), math.log(0.8))
    spike_matches = jnp.arange(TOKEN_COUNT, dtype=jnp.int32)[None, None, :] == spike_position[:, :, None]
    event_spikes = jnp.sum(jnp.where(spike_matches, spike_penalty[:, :, None], 0.0), axis=1)
    return (forget_rates + event_spikes).astype(jnp.float32)


def strengthened(values, stream_key, source, target, blocks, factor):
    def block_of(axis_at):
        return (jnp.arange(values.shape[axis_at]) // (values.shape[axis_at] // blocks)).reshape((-1,) + (1,) * (values.ndim - 1 - axis_at))

    one_side = jax.random.permutation(stream_key, blocks)[block_of(target)]
    second = (block_of(target) + blocks // 2) % blocks
    return jnp.where((block_of(source) == one_side) | (block_of(source) == second), factor * values, values)


def levels(rng, extent, pieces, low, top_value):
    gain, own = 1.0, jax.random.fold_in(rng, 6)
    for axis_at, shards_of in pieces:
        steps = jnp.exp(jax.random.uniform(jax.random.fold_in(own, axis_at), (shards_of,), jnp.float32, low / len(pieces), top_value / len(pieces)))
        gain = gain * jnp.repeat(steps, extent[axis_at] // shards_of).reshape([-1 if axis == axis_at else 1 for axis in range(len(extent))])
    return gain


def scatter_about(own_key, shape, deviation, bound, shards=(), kind=jnp.bfloat16):
    drawn = jax.random.normal(own_key, shape, jnp.float32) * deviation
    if len(shards) > 0:
        drawn = levels(own_key, shape, shards, -0.22, 0.18) * drawn
    return jnp.clip(drawn, min=-bound, max=bound).astype(kind)


def noise_with(stream_key, extent, scale, reach, cuts, heavy, kind=jnp.bfloat16):
    values = scale * jax.random.normal(stream_key, extent, jnp.float32)
    if cuts:
        values = values * levels(stream_key, extent, cuts, -0.22, 0.18)
    return jnp.clip(strengthened(values, jax.random.fold_in(stream_key, 3), *heavy), -reach, reach).astype(kind)


def setup_inputs(seed: int = 0) -> dict:
    arg_keys = jax.random.split(jax.random.key(seed), 12)
    events = noise_with(arg_keys[0], (TOKEN_COUNT, D), 1.0, 8.0, ((0, 16),), (0, 1, 16, 2.0))
    ssm_input = scatter_about(arg_keys[1], (TOKEN_COUNT, HEAD_TOTAL * HEAD_DIM), 0.25, 1.5, ((0, 16), (1, 2)))
    gate_input = scatter_about(arg_keys[2], (TOKEN_COUNT, HEAD_TOTAL * HEAD_DIM), 1.0, 6.0, ((0, 16), (1, 2)))
    grad_out = scatter_about(arg_keys[3], (TOKEN_COUNT, HEAD_TOTAL * HEAD_DIM), 0.003, 0.015625, ((0, 16), (1, 2)))
    shared_b = scatter_about(arg_keys[4], (TOKEN_COUNT, STATE), 1.0, 6.0, ((0, 16),))
    shared_c = scatter_about(arg_keys[5], (TOKEN_COUNT, STATE), 1.0, 6.0, ((0, 16),))
    log_decay = draw_log_decay(jax.random.fold_in(arg_keys[11], 71), 0)
    entry_state = scatter_about(arg_keys[7], (BLOCKS, HEAD_TOTAL, STATE, HEAD_DIM), 8.0, 48.0, ((0, 16), (1, 2)), jnp.float32)
    w_gate = scatter_about(arg_keys[8], (D, HEAD_TOTAL * HEAD_DIM), D ** -0.5, 0.1875, ((1, 2),))
    w_value = scatter_about(arg_keys[9], (D, HEAD_TOTAL * HEAD_DIM), D ** -0.5, 0.1875, ((1, 2),))
    w_shared = scatter_about(arg_keys[10], (D, 2 * STATE), D ** -0.5, 0.1875, ((1, 2),))
    return dict(events=events, ssm_input=ssm_input, gate_input=gate_input, grad_out=grad_out, shared_b=shared_b, shared_c=shared_c, log_decay=log_decay, entry_state=entry_state, w_gate=w_gate, w_value=w_value, w_shared=w_shared)


highest = lax.Precision.HIGHEST

def ssd_partials(ssm_input, gate_input, grad_out, shared_b, shared_c, log_decay, entry, block_len):
    head_count, length = log_decay.shape
    head_width = ssm_input.shape[1] // head_count
    span_count = length // block_len
    values_f = ssm_input.astype(jnp.float32).reshape(span_count, block_len, head_count, head_width)
    gates_f = gate_input.astype(jnp.float32).reshape(span_count, block_len, head_count, head_width)
    grad_f = grad_out.astype(jnp.float32).reshape(span_count, block_len, head_count, head_width)
    shared_bf = shared_b.astype(jnp.float32).reshape(span_count, block_len, shared_b.shape[1])
    shared_cf = shared_c.astype(jnp.float32).reshape(span_count, block_len, shared_c.shape[1])
    cumlog = jnp.cumsum(log_decay.reshape(head_count, span_count, block_len), axis=2)
    totals = cumlog[:, :, -1]
    causal = jnp.arange(block_len)[:, None] >= jnp.arange(block_len)[None, :]
    spread = cumlog[:, :, :, None] - cumlog[:, :, None, :]
    decay_mat = jnp.where(causal, jnp.exp(jnp.minimum(spread, 0.0)), 0.0)
    scores = jnp.einsum('ktn,ksn->kts', shared_cf, shared_bf, precision=highest)
    weighted = decay_mat * scores[None]
    to_end = jnp.exp(totals[:, :, None] - cumlog).transpose(1, 2, 0)
    from_start = jnp.exp(cumlog).transpose(1, 2, 0)
    scaled_x = values_f * to_end[..., None]
    local_states = jnp.einsum('ksn,kshp->khnp', shared_bf, scaled_x, precision=highest)
    span_decay = jnp.exp(totals).T

    def forward_step(running, inputs):
        decay_k, local_k = inputs
        return (decay_k[:, None, None] * running + local_k, running)
    _, entries = lax.scan(forward_step, entry, (span_decay, local_states))
    ssm_out = jnp.einsum('hkts,kshp->kthp', weighted, values_f, precision=highest)
    ssm_out = ssm_out + from_start[..., None] * jnp.einsum('ktn,khnp->kthp', shared_cf, entries, precision=highest)
    gate_sig = jax.nn.sigmoid(gates_f)
    grad_y = grad_f * gates_f * gate_sig
    grad_z = grad_f * ssm_out * gate_sig * (1.0 + gates_f * (1.0 - gate_sig))
    products = decay_mat * jnp.einsum('kthp,kshp->hkts', grad_y, values_f, precision=highest)
    scaled_dy = grad_y * from_start[..., None]
    grad_c = jnp.einsum('hkts,ksn->ktn', products, shared_bf, precision=highest)
    grad_c = grad_c + jnp.einsum('kthp,khnp->ktn', scaled_dy, entries, precision=highest)
    grad_b = jnp.einsum('hkst,ksn->ktn', products, shared_cf, precision=highest)
    grad_x = jnp.einsum('hkst,kshp->kthp', weighted, grad_y, precision=highest)
    block_terms = jnp.einsum('ksn,kshp->khnp', shared_cf, scaled_dy, precision=highest)

    def backward_step(running, inputs):
        decay_k, term_k = inputs
        return (term_k + decay_k[:, None, None] * running, running)
    block_sum, later_sums = lax.scan(backward_step, jnp.zeros_like(entry), (span_decay, block_terms), reverse=True)
    block_log = lax.optimization_barrier(jnp.sum(totals, axis=1))
    suffix = block_log[None, :] - jnp.cumsum(totals, axis=1).T
    grad_z_out = grad_z.reshape(length, head_count * head_width).astype(jnp.bfloat16)
    return (grad_z_out, grad_x, grad_b, grad_c, later_sums, suffix, to_end, scaled_x, shared_bf, block_sum, block_log)

def finish_block(partials, incoming):
    grad_z_out, grad_x, grad_b, grad_c, later_sums, suffix, to_end, scaled_x, shared_bf, block_sum, block_log = partials
    carried = later_sums + jnp.exp(suffix)[:, :, None, None] * incoming[None]
    grad_x = grad_x + to_end[..., None] * jnp.einsum('ktn,khnp->kthp', shared_bf, carried, precision=highest)
    grad_b = grad_b + jnp.einsum('kthp,khnp->ktn', scaled_x, carried, precision=highest)
    length = grad_z_out.shape[0]
    grad_x_out = grad_x.reshape(length, grad_z_out.shape[1]).astype(jnp.bfloat16)
    grad_bc = jnp.concatenate([grad_b.reshape(length, -1), grad_c.reshape(length, -1)], axis=1)
    return (grad_z_out, grad_x_out, grad_bc)

def reference(events, ssm_input, gate_input, grad_out, shared_b, shared_c, log_decay, entry_state, w_gate, w_value, w_shared):
    blocks = TOKEN_COUNT // L_DEV

    def by_block(array):
        return array.reshape(blocks, L_DEV, array.shape[1])
    decays = log_decay.reshape(HEAD_TOTAL, blocks, L_DEV).transpose(1, 0, 2)

    def block_step(incoming, inputs):
        part_x, part_g, part_o, part_b, part_c, part_d, part_e = inputs
        partials = ssd_partials(part_x, part_g, part_o, part_b, part_c, part_d, part_e, SPAN)
        outputs = finish_block(partials, incoming)
        return (partials[9] + jnp.exp(partials[10])[:, None, None] * incoming, outputs)
    initial = jnp.zeros((HEAD_TOTAL, STATE, HEAD_DIM), jnp.float32)
    stacked = (by_block(ssm_input), by_block(gate_input), by_block(grad_out), by_block(shared_b), by_block(shared_c), decays, entry_state)
    _, (grad_z, grad_x, grad_bc) = lax.scan(block_step, initial, stacked, reverse=True)
    grad_z = grad_z.reshape(TOKEN_COUNT, HEAD_TOTAL * HEAD_DIM)
    grad_x = grad_x.reshape(TOKEN_COUNT, HEAD_TOTAL * HEAD_DIM)
    grad_bc = grad_bc.reshape(TOKEN_COUNT, 2 * STATE).astype(jnp.bfloat16)
    head_cols = GROUP_HEADS * HEAD_DIM
    shared_cols = 2 * STATE // N_HEAD
    summed = jnp.zeros((TOKEN_COUNT, D), jnp.float32)
    for group in range(N_HEAD):
        low_head = group * head_cols
        high_head = low_head + head_cols
        low_shared = group * shared_cols
        high_shared = low_shared + shared_cols
        partial_value = jnp.dot(grad_z[:, low_head:high_head], w_gate[:, low_head:high_head].T, preferred_element_type=jnp.float32)
        partial_value = partial_value + jnp.dot(grad_x[:, low_head:high_head], w_value[:, low_head:high_head].T, preferred_element_type=jnp.float32)
        partial_value = partial_value + jnp.dot(grad_bc[:, low_shared:high_shared], w_shared[:, low_shared:high_shared].T, preferred_element_type=jnp.float32)
        summed = summed + lax.optimization_barrier(partial_value.astype(jnp.bfloat16)).astype(jnp.float32)
    grad_input = summed.astype(jnp.bfloat16)
    norm_scale = 1.0 / math.sqrt(TOKEN_COUNT)
    grad_w_gate = jnp.dot(events.T, grad_z, preferred_element_type=jnp.float32) * norm_scale
    grad_w_value = jnp.dot(events.T, grad_x, preferred_element_type=jnp.float32) * norm_scale
    grad_w_shared = jnp.dot(events.T, grad_bc, preferred_element_type=jnp.float32) * norm_scale
    return (grad_input, grad_w_gate, grad_w_value, grad_w_shared)
```

```python
import math

import jax
import jax.numpy as jnp
from jax import lax
from jax.sharding import PartitionSpec as P

SPAN = 256


highest = lax.Precision.HIGHEST


def entering(block_log, block_sum, axis):
    count = lax.axis_size(axis)
    place = lax.axis_index(axis)
    logs = lax.all_gather(block_log, axis)
    sums = lax.all_gather(block_sum.astype(jnp.bfloat16), axis)
    index = jnp.arange(count)[:, None]
    between = ((index > index.T) & (index.T > place))[:, :, None]
    exponent = jnp.sum(jnp.where(between, logs[None], 0.0), axis=1)
    weight = jnp.where(index > place, jnp.exp(exponent), 0.0)
    return jnp.sum(weight[:, :, None, None] * sums.astype(jnp.float32), axis=0)


def ssd_partials(ssm_input, gate_input, grad_out, shared_b, shared_c, log_decay, entry, block_len):
    head_count, length = log_decay.shape
    head_width = ssm_input.shape[1] // head_count
    span_count = length // block_len
    values_f = ssm_input.astype(jnp.float32).reshape(span_count, block_len, head_count, head_width)
    gates_f = gate_input.astype(jnp.float32).reshape(span_count, block_len, head_count, head_width)
    grad_f = grad_out.astype(jnp.float32).reshape(span_count, block_len, head_count, head_width)
    shared_bf = shared_b.astype(jnp.float32).reshape(span_count, block_len, shared_b.shape[1])
    shared_cf = shared_c.astype(jnp.float32).reshape(span_count, block_len, shared_c.shape[1])
    cumlog = jnp.cumsum(log_decay.reshape(head_count, span_count, block_len), axis=2)
    totals = cumlog[:, :, -1]
    causal = jnp.arange(block_len)[:, None] >= jnp.arange(block_len)[None, :]
    spread = cumlog[:, :, :, None] - cumlog[:, :, None, :]
    decay_mat = jnp.where(causal, jnp.exp(jnp.minimum(spread, 0.0)), 0.0)
    shared_c_blocks = shared_c.reshape(span_count, block_len, shared_c.shape[1])
    shared_b_blocks = shared_b.reshape(span_count, block_len, shared_b.shape[1])
    scores = jnp.einsum(
        "ktn,ksn->kts", shared_c_blocks, shared_b_blocks, preferred_element_type=jnp.float32
    )
    weighted = decay_mat * scores[None]
    to_end = jnp.exp(totals[:, :, None] - cumlog).transpose(1, 2, 0)
    from_start = jnp.exp(cumlog).transpose(1, 2, 0)
    scaled_x = values_f * to_end[..., None]
    local_states = jnp.einsum("ksn,kshp->khnp", shared_bf, scaled_x, precision=highest)
    span_decay = jnp.exp(totals).T

    def forward_step(running, inputs):
        decay_k, local_k = inputs
        return (decay_k[:, None, None] * running + local_k, running)

    _, entries = lax.scan(forward_step, entry, (span_decay, local_states))
    ssm_out = jnp.einsum("hkts,kshp->kthp", weighted, values_f, precision=highest)
    ssm_out = ssm_out + from_start[..., None] * jnp.einsum(
        "ktn,khnp->kthp", shared_cf, entries, precision=highest
    )
    gate_sig = jax.nn.sigmoid(gates_f)
    grad_y = grad_f * gates_f * gate_sig
    grad_z = grad_f * ssm_out * gate_sig * (1.0 + gates_f * (1.0 - gate_sig))
    products = decay_mat * jnp.einsum("kthp,kshp->hkts", grad_y, values_f, precision=highest)
    scaled_dy = grad_y * from_start[..., None]
    grad_c = jnp.einsum("hkts,ksn->ktn", products, shared_bf, precision=highest)
    grad_c = grad_c + jnp.einsum("kthp,khnp->ktn", scaled_dy, entries, precision=highest)
    grad_b = jnp.einsum("hkst,ksn->ktn", products, shared_cf, precision=highest)
    grad_x = jnp.einsum("hkst,kshp->kthp", weighted, grad_y, precision=highest)
    block_terms = jnp.einsum("ksn,kshp->khnp", shared_cf, scaled_dy, precision=highest)

    def backward_step(running, inputs):
        decay_k, term_k = inputs
        return (term_k + decay_k[:, None, None] * running, running)

    block_sum, later_sums = lax.scan(
        backward_step, jnp.zeros_like(entry), (span_decay, block_terms), reverse=True
    )
    block_log = jnp.sum(totals, axis=1)
    suffix = block_log[None, :] - jnp.cumsum(totals, axis=1).T
    grad_z_out = grad_z.reshape(length, head_count * head_width).astype(jnp.bfloat16)
    return (
        grad_z_out,
        grad_x,
        grad_b,
        grad_c,
        later_sums,
        suffix,
        to_end,
        scaled_x,
        shared_bf,
        block_sum,
        block_log,
    )


def finish_block(partials, incoming):
    (
        grad_z_out,
        grad_x,
        grad_b,
        grad_c,
        later_sums,
        suffix,
        to_end,
        scaled_x,
        shared_bf,
        block_sum,
        block_log,
    ) = partials
    carried = later_sums + jnp.exp(suffix)[:, :, None, None] * incoming[None]
    grad_x = grad_x + to_end[..., None] * jnp.einsum(
        "ktn,khnp->kthp", shared_bf, carried, precision=highest
    )
    grad_b = grad_b + jnp.einsum("kthp,khnp->ktn", scaled_x, carried, precision=highest)
    length = grad_z_out.shape[0]
    grad_x_out = grad_x.reshape(length, grad_z_out.shape[1]).astype(jnp.bfloat16)
    grad_bc = jnp.concatenate([grad_b.reshape(length, -1), grad_c.reshape(length, -1)], axis=1)
    return (grad_z_out, grad_x_out, grad_bc)


def times_rows(left, weights):
    return lax.dot_general(
        left, weights, (((1,), (1,)), ((), ())), preferred_element_type=jnp.float32
    )


def row_term(events, projected, norm_scale):
    return (
        lax.dot_general(
            events, projected, (((0,), (0,)), ((), ())), preferred_element_type=jnp.float32
        )
        * norm_scale
    )


def per_device(
    events,
    ssm_input,
    gate_input,
    grad_out,
    shared_b,
    shared_c,
    log_decay,
    entry_state,
    w_gate,
    w_value,
    w_shared,
):
    partials = ssd_partials(
        ssm_input, gate_input, grad_out, shared_b, shared_c, log_decay, entry_state[0], SPAN
    )
    grad_z = partials[0]
    block_sum = partials[9]
    block_log = partials[10]

    incoming = entering(block_log, block_sum, "ctx")
    grad_z, grad_x, grad_bc_part = finish_block(partials, incoming)
    grad_bc = lax.psum_scatter(grad_bc_part, "head", scatter_dimension=1, tiled=True).astype(
        jnp.bfloat16
    )
    input_part = (
        times_rows(grad_z, w_gate) + times_rows(grad_x, w_value) + times_rows(grad_bc, w_shared)
    )
    grad_input = lax.psum_scatter(
        input_part.astype(jnp.bfloat16), "head", scatter_dimension=1, tiled=True
    )
    norm_scale = 1.0 / math.sqrt(events.shape[0] * lax.axis_size("ctx"))
    head_cols = grad_z.shape[1]
    projected = jnp.concatenate([grad_z, grad_x, grad_bc], axis=1)
    reduced = lax.psum_scatter(
        row_term(events, projected, norm_scale).astype(jnp.bfloat16),
        "ctx",
        scatter_dimension=0,
        tiled=True,
    ).astype(jnp.float32)
    grad_w_gate = reduced[:, :head_cols]
    grad_w_value = reduced[:, head_cols : 2 * head_cols]
    grad_w_shared = reduced[:, 2 * head_cols :]
    return (grad_input, grad_w_gate, grad_w_value, grad_w_shared)


def solution(mesh):
    placed = (
        P("ctx", None),
        P("ctx", "head"),
        P("ctx", "head"),
        P("ctx", "head"),
        P("ctx", None),
        P("ctx", None),
        P("head", "ctx"),
        P("ctx", "head", None, None),
        P(None, "head"),
        P(None, "head"),
        P(None, "head"),
    )
    return jax.shard_map(
        per_device,
        mesh=mesh,
        in_specs=placed,
        out_specs=(P("ctx", "head"), P("ctx", "head"), P("ctx", "head"), P("ctx", "head")),
        check_vma=False,
    )
```

```python
import functools
import math

import jax
import jax.numpy as jnp
from jax import lax
from jax.experimental import pallas as pl
from jax.experimental.pallas import tpu as pltpu
from jax.sharding import PartitionSpec as P

F32 = jnp.float32
BF16 = jnp.bfloat16
HIGHEST = lax.Precision.HIGHEST
MESH = pl.DeviceIdType.MESH
LANES = 128


def dot(a, b, dims=(1, 0), precision=None):
    return lax.dot_general(
        a,
        b,
        (((dims[0],), (dims[1],)), ((), ())),
        preferred_element_type=F32,
        precision=precision,
    )


def split_orders(bits):
    plain = list(range(bits))
    swapped = list(plain)
    if bits >= 3:
        swapped[1], swapped[2] = swapped[2], swapped[1]
    return plain, swapped


def mixer_kernel(cfg, *refs):
    n_ctx, n_head, widths, shared_cols, scale = cfg
    bits = n_ctx.bit_length() - 1
    chunks = len(widths)
    refs = list(refs)
    (ev, x_in, gate, gout, b_in, c_in, ld_in, ent, wg, wv, ws) = refs[:11]
    (o_in, o_g, o_v, o_s) = refs[11:15]
    it = iter(refs[15:])
    cumx, rowc, dyb, sdy, entb, gz, gxp, gxb, psum, acc, evt = [next(it) for _ in range(11)]
    tf, tsend, dsend, inc = [next(it) for _ in range(4)]
    crecv = [next(it) for _ in range(bits)]
    drecv = [next(it) for _ in range(bits)]
    csend = [next(it) for _ in range(bits - 1)]
    dnext = [next(it) for _ in range(bits - 1)]
    ifar = next(it)
    held = [[next(it) for _ in range(bits)] for _ in range(chunks)]
    land = [[next(it) for _ in range(bits)] for _ in range(chunks)]
    bcs, bcr, gis, gir = [next(it) for _ in range(4)]
    c_ss, c_rs, d_ss, d_rs, w_ss, w_rs, b_ss, b_rs, g_ss, g_rs = [next(it) for _ in range(10)]

    length, cols = x_in.shape
    state = b_in.shape[1]
    heads = ld_in.shape[0]
    width = cols // heads
    half = cols // 2
    rows = ev.shape[1] // n_ctx
    out_cols = ev.shape[1] // n_head
    pairs = cols // LANES
    per_pair = LANES // width

    me = lax.axis_index("ctx")
    hid = lax.axis_index("head")
    bit = [lax.rem(me // (1 << b), 2) for b in range(bits)]
    partner = [me + (1 - 2 * bit[b]) * (1 << b) for b in range(bits)]
    peers = [lax.rem(hid + r, n_head) for r in range(1, n_head)]
    core = bit[0]
    started = []

    def send(src, dst, ss, rs, ctx_id, head_id):
        copy = pltpu.make_async_remote_copy(
            src_ref=src,
            dst_ref=dst,
            send_sem=ss,
            recv_sem=rs,
            device_id=(ctx_id, head_id),
            device_id_type=MESH,
        )
        copy.start()
        started.append(copy)
        return copy

    barrier = pltpu.get_barrier_semaphore()
    for p in partner:
        pl.semaphore_signal(barrier, inc=1, device_id=(p, hid), device_id_type=MESH)
    for p in peers:
        pl.semaphore_signal(barrier, inc=1, device_id=(me, p), device_id_type=MESH)

    t_id = lax.broadcasted_iota(jnp.int32, (length, length), 0)
    s_id = lax.broadcasted_iota(jnp.int32, (length, length), 1)
    tril = t_id >= s_id
    triu = t_id <= s_id
    ld = ld_in[...]
    colcum = dot(tril.astype(F32), ld, (1, 1), HIGHEST)
    pick = (
        lax.broadcasted_iota(jnp.int32, (heads, cols), 1) // width
        == lax.broadcasted_iota(jnp.int32, (heads, cols), 0)
    ).astype(F32)
    cumx[...] = dot(colcum, pick, (1, 0), HIGHEST)
    rowc[...] = dot(ld, triu.astype(F32), (1, 0), HIGHEST)
    total = cumx[length - 1 : length, :]

    def at(k):
        return pl.ds(pl.multiple_of(k * LANES, LANES), LANES)

    def before(k, carry):
        sl = at(k)
        g = gate[:, sl].astype(F32)
        dy = gout[:, sl].astype(F32) * g * (1.0 / (1.0 + jnp.exp(-g)))
        dyb[:, sl] = dy.astype(BF16)
        sdy[:, sl] = (dy * jnp.exp(cumx[:, sl])).astype(BF16)
        return carry

    lax.fori_loop(0, pairs, before, 0)
    terms = dot(c_in[...], sdy[...], (0, 0))
    decays = jnp.broadcast_to(jnp.exp(total), (8, cols))
    for h in range(2):
        part = terms[:, h * half : (h + 1) * half]
        tf[h] = part
        tsend[h] = part.astype(BF16)
        dsend[h] = decays[:, h * half : (h + 1) * half]

    pl.semaphore_wait(barrier, bits + n_head - 1)

    flight = {}
    flight[0] = (
        send(tsend.at[1 - core], crecv[0], c_ss.at[0], c_rs.at[0], partner[0], hid),
        send(dsend.at[1 - core], drecv[0], d_ss.at[0], d_rs.at[0], partner[0], hid),
    )
    chain = {}

    def carry_step(k):
        if k == bits:
            flight[bits].wait_recv()
            return
        for copy in flight[k]:
            copy.wait_recv()
        other, other_d = crecv[k][...].astype(F32), drecv[k][0:1, :]
        early = bit[k] == 0
        if k == 0:
            mine, mine_d = tf[core], dsend[core][0:1, :]
            first = jnp.where(early, mine, other)
            last = jnp.where(early, other, mine)
            first_d = jnp.where(early, mine_d, other_d)
            last_d = jnp.where(early, other_d, mine_d)
            chain["last"], chain["last_d"] = last, last_d
            chain["t"] = first + first_d * last
            chain["d"] = first_d * last_d
            chain["x"] = jnp.zeros_like(last)
            chain["q"] = jnp.ones_like(last_d)
        else:
            t, d = chain["t"], chain["d"]
            chain["x"] = jnp.where(early, chain["x"] + chain["q"] * other, chain["x"])
            chain["q"] = jnp.where(early, chain["q"] * other_d, chain["q"])
            chain["t"] = jnp.where(early, t + d * other, other + other_d * t)
            chain["d"] = d * other_d
        if k < bits - 1:
            csend[k][...] = chain["t"].astype(BF16)
            dnext[k][...] = jnp.broadcast_to(chain["d"], (8, half))
            flight[k + 1] = (
                send(csend[k], crecv[k + 1], c_ss.at[k + 1], c_rs.at[k + 1], partner[k + 1], hid),
                send(dnext[k], drecv[k + 1], d_ss.at[k + 1], d_rs.at[k + 1], partner[k + 1], hid),
            )
        else:
            x = chain["x"]
            deeper = chain["last"] + chain["last_d"] * x
            ifar[...] = jnp.where(core == 0, x, deeper).astype(BF16)
            flight[bits] = send(
                ifar, inc.at[core], c_ss.at[bits], c_rs.at[bits], partner[0], hid
            )
            inc[core] = jnp.where(core == 0, deeper, x).astype(BF16)

    orders = split_orders(bits)
    rs_flight = {}

    def rs_send(c, k):
        order = orders[c % 2]
        b = order[k]
        count = n_ctx >> (k + 1)
        rs_flight[c, k] = send(
            held[c][k].at[pl.ds((1 - bit[b]) * count, count)],
            land[c][k],
            w_ss.at[c * bits + k],
            w_rs.at[c * bits + k],
            partner[b],
            hid,
        )

    def rs_begin(c, values):
        order = orders[c % 2]
        tile = min(256, ev.shape[1])
        for start in range(0, ev.shape[1], tile):
            part = dot(evt[start : start + tile, :], values).astype(BF16)
            for j in range(tile // rows):
                index = start // rows + j
                place = 0
                for k, b in enumerate(order):
                    place += ((index >> b) & 1) << (bits - 1 - k)
                held[c][0][place] = part[j * rows : (j + 1) * rows, :]
        rs_send(c, 0)

    outs = []

    def rs_step(c, k):
        order = orders[c % 2]
        b = order[k]
        count = n_ctx >> (k + 1)
        rs_flight[c, k].wait_recv()
        kept = held[c][k][pl.ds(bit[b] * count, count)].astype(F32) + land[c][k][...].astype(F32)
        if k < bits - 1:
            held[c][k + 1][...] = kept.astype(BF16)
            rs_send(c, k + 1)
        else:
            out, low, high = outs[c]
            out[:, low:high] = kept[0] * scale

    per_kind = (chunks - 1) // 2
    step = cols // per_kind
    for out in (o_g, o_v):
        for j in range(per_kind):
            outs.append((out, j * step, (j + 1) * step))
    outs.append((o_s, 0, widths[-1]))

    scores = dot(c_in[...], b_in[...], (1, 1))
    scores_t = dot(b_in[...], c_in[...], (1, 1))
    entb[...] = ent[...].astype(BF16)
    psum[...] = jnp.zeros_like(psum)
    lane = lax.broadcasted_iota(jnp.int32, (length, LANES), 1) // width

    def pair(k, carry):
        sl = at(k)
        x = x_in[:, sl]
        cum = cumx[:, sl]
        dyv = dyb[:, sl]
        dyf = dyv.astype(F32)
        y = jnp.exp(cum) * dot(c_in[...], entb[sl, :], (1, 1))
        gx = jnp.zeros((length, LANES), F32)
        both = psum[...]
        for q in range(per_pair):
            col = cum[:, q * width : q * width + 1]
            row = rowc[pl.ds(k * per_pair + q, 1), :]
            gap = col - row
            decay = jnp.where(tril, jnp.exp(jnp.minimum(gap, 0.0)), 0.0)
            decay_t = jnp.where(triu, jnp.exp(jnp.minimum(-gap, 0.0)), 0.0)
            own = lane == q
            y = y + jnp.where(own, dot((decay * scores).astype(BF16), x), 0.0)
            gx = gx + jnp.where(own, dot((decay_t * scores_t).astype(BF16), dyv), 0.0)
            both = both + decay * dot(jnp.where(own, dyf, 0.0).astype(BF16), x, (1, 1))
        psum[...] = both
        gxp[:, sl] = gx
        g = gate[:, sl].astype(F32)
        sig = 1.0 / (1.0 + jnp.exp(-g))
        gz[:, sl] = (gout[:, sl].astype(F32) * y * sig * (1.0 + g * (1.0 - sig))).astype(BF16)
        return carry

    cuts = [0, pairs // 4, pairs // 2, pairs]

    def some_pairs(i):
        if cuts[i + 1] > cuts[i]:
            lax.fori_loop(cuts[i], cuts[i + 1], pair, 0)

    evt[...] = ev[...].T
    some_pairs(0)
    carry_step(0)
    some_pairs(1)
    carry_step(1)
    some_pairs(2)
    carry_step(2)
    for c in range(per_kind):
        rs_begin(c, gz[:, c * step : (c + 1) * step])
    for k in range(3, bits):
        carry_step(k)
    acc[...] = dot(gz[...], wg[...], (1, 1))
    grad_c = dot(psum[...].astype(BF16), b_in[...]) + dot(sdy[...], entb[...])
    grad_b = dot(psum[...].T.astype(BF16), c_in[...])
    for c in range(per_kind):
        rs_step(c, 0)
    carry_step(bits)

    for h in range(2):
        cut = slice(h * half, (h + 1) * half)
        to_end = jnp.exp(total[:, cut] - cumx[:, cut])
        gxb[:, cut] = (gxp[:, cut] + to_end * dot(b_in[...], inc[h])).astype(BF16)
        scaled = (x_in[:, cut].astype(F32) * to_end).astype(BF16)
        grad_b = grad_b + dot(scaled, inc[h], (1, 1))
    bcs[:, 0:state] = grad_b.astype(BF16)
    bcs[:, state : 2 * state] = grad_c.astype(BF16)
    bc_copies = [
        send(bcs, bcr.at[r], b_ss.at[r], b_rs.at[r], me, p) for r, p in enumerate(peers)
    ]
    for c in range(per_kind):
        rs_begin(per_kind + c, gxb[:, c * step : (c + 1) * step])
    for c in range(per_kind):
        rs_step(c, 1)
    acc[...] += dot(gxb[...], wv[...], (1, 1))
    grad_bc = jnp.concatenate([grad_b, grad_c], axis=1)
    for r, copy in enumerate(bc_copies):
        copy.wait_recv()
        grad_bc = grad_bc + bcr[r].astype(F32)
    sel = (
        lax.broadcasted_iota(jnp.int32, (2 * state, widths[-1]), 0)
        == lax.broadcasted_iota(jnp.int32, (2 * state, widths[-1]), 1) + hid * shared_cols
    ) & (lax.broadcasted_iota(jnp.int32, (2 * state, widths[-1]), 1) < shared_cols)
    shared = dot(grad_bc.astype(BF16), sel.astype(F32).astype(BF16)).astype(BF16)
    rs_begin(chunks - 1, shared)
    full = acc[...] + dot(shared, ws[...], (1, 1))
    for j in range(n_head):
        gis[j] = full[:, j * out_cols : (j + 1) * out_cols].astype(BF16)
    gi_copies = [
        send(gis.at[p], gir.at[r], g_ss.at[r], g_rs.at[r], me, p) for r, p in enumerate(peers)
    ]
    value_chunks = range(per_kind, chunks)
    for k in range(bits):
        for c in value_chunks:
            rs_step(c, k)
        if k + 2 < bits:
            for c in range(per_kind):
                rs_step(c, k + 2)
    grad_in = gis[hid].astype(F32)
    for r, copy in enumerate(gi_copies):
        copy.wait_recv()
        grad_in = grad_in + gir[r].astype(F32)
    o_in[...] = grad_in.astype(BF16)
    for copy in started:
        copy.wait_send()


def per_device(
    n_ctx,
    n_head,
    events,
    ssm_input,
    gate_input,
    grad_out,
    shared_b,
    shared_c,
    log_decay,
    entry_state,
    w_gate,
    w_value,
    w_shared,
):
    length, cols = ssm_input.shape
    depth = events.shape[1]
    state = shared_b.shape[1]
    shared_cols = w_shared.shape[1]
    shared_wide = -(-shared_cols // LANES) * LANES
    if shared_wide > shared_cols:
        w_shared = jnp.pad(w_shared, ((0, 0), (0, shared_wide - shared_cols)))
    bits = n_ctx.bit_length() - 1
    rows = depth // n_ctx
    per_kind = 2
    widths = [cols // per_kind] * (2 * per_kind) + [shared_wide]
    half = cols // 2
    entry = entry_state[0].transpose(0, 2, 1).reshape(cols, state)
    scale = 1.0 / math.sqrt(length * n_ctx)
    v = pltpu.VMEM
    dma = pltpu.SemaphoreType.DMA
    peers = n_head - 1
    scratch = [
        v((length, cols), F32),
        v((log_decay.shape[0], length), F32),
        v((length, cols), BF16),
        v((length, cols), BF16),
        v((cols, state), BF16),
        v((length, cols), BF16),
        v((length, cols), F32),
        v((length, cols), BF16),
        v((length, length), F32),
        v((length, depth), F32),
        v((depth, length), BF16),
        v((2, state, half), F32),
        v((2, state, half), BF16),
        v((2, 8, half), F32),
        v((2, state, half), BF16),
    ]
    scratch += [v((state, half), BF16) for _ in range(bits)]
    scratch += [v((8, half), F32) for _ in range(bits)]
    scratch += [v((state, half), BF16) for _ in range(bits - 1)]
    scratch += [v((8, half), F32) for _ in range(bits - 1)]
    scratch += [v((state, half), BF16)]
    for w in widths:
        scratch += [v((n_ctx >> k, rows, w), BF16) for k in range(bits)]
    for w in widths:
        scratch += [v((n_ctx >> (k + 1), rows, w), BF16) for k in range(bits)]
    scratch += [
        v((length, 2 * state), BF16),
        v((peers, length, 2 * state), BF16),
        v((n_head, length, depth // n_head), BF16),
        v((peers, length, depth // n_head), BF16),
        dma((bits + 1,)),
        dma((bits + 1,)),
        dma((bits,)),
        dma((bits,)),
        dma((len(widths) * bits,)),
        dma((len(widths) * bits,)),
        dma((peers,)),
        dma((peers,)),
        dma((peers,)),
        dma((peers,)),
    ]
    whole = pl.BlockSpec(memory_space=pltpu.VMEM)
    flops = 2 * length * (5 * state * cols + 3 * length * cols + 4 * depth * cols)
    grad_input, grad_w_gate, grad_w_value, grad_w_shared = pl.pallas_call(
        functools.partial(mixer_kernel, (n_ctx, n_head, widths, shared_cols, scale)),
        out_shape=(
            jax.ShapeDtypeStruct((length, depth // n_head), BF16),
            jax.ShapeDtypeStruct((rows, cols), F32),
            jax.ShapeDtypeStruct((rows, cols), F32),
            jax.ShapeDtypeStruct((rows, shared_wide), F32),
        ),
        in_specs=[whole] * 11,
        out_specs=(whole,) * 4,
        scratch_shapes=scratch,
        compiler_params=pltpu.CompilerParams(
            collective_id=0, has_side_effects=True, vmem_limit_bytes=58 * 1024 * 1024
        ),
        cost_estimate=pl.CostEstimate(
            flops=flops, bytes_accessed=8 * 1024 * 1024, transcendentals=length * length * 32
        ),
        name="mixer",
    )(
        events,
        ssm_input,
        gate_input,
        grad_out,
        shared_b,
        shared_c,
        log_decay,
        entry,
        w_gate,
        w_value,
        w_shared,
    )
    return (grad_input, grad_w_gate, grad_w_value, grad_w_shared[:, :shared_cols])


def solution(mesh):
    placed = (
        P("ctx", None),
        P("ctx", "head"),
        P("ctx", "head"),
        P("ctx", "head"),
        P("ctx", None),
        P("ctx", None),
        P("head", "ctx"),
        P("ctx", "head", None, None),
        P(None, "head"),
        P(None, "head"),
        P(None, "head"),
    )
    return jax.shard_map(
        functools.partial(per_device, mesh.shape["ctx"], mesh.shape["head"]),
        mesh=mesh,
        in_specs=placed,
        out_specs=(P("ctx", "head"), P("ctx", "head"), P("ctx", "head"), P("ctx", "head")),
        check_vma=False,
    )
```

```python
import functools
import math

import jax
import jax.numpy as jnp
from jax import lax
from jax.experimental import pallas as pl
from jax.experimental.pallas import tpu as pltpu
from jax.sharding import PartitionSpec as P

F32 = jnp.float32
BF16 = jnp.bfloat16
HIGHEST = lax.Precision.HIGHEST
MESH = pl.DeviceIdType.MESH
LANES = 128


def dot(a, b, dims=(1, 0), precision=None):
    return lax.dot_general(
        a,
        b,
        (((dims[0],), (dims[1],)), ((), ())),
        preferred_element_type=F32,
        precision=precision,
    )


def split_orders(bits):
    plain = list(range(bits))
    swapped = list(plain)
    if bits >= 3:
        swapped[1], swapped[2] = swapped[2], swapped[1]
    return plain, swapped


def mixer_kernel(cfg, *refs):
    n_ctx, n_head, widths, shared_cols = cfg
    bits = n_ctx.bit_length() - 1
    chunks = len(widths)
    refs = list(refs)
    (ev_h, x_in, gate, gout, b_in, c_in, ld_in, ent_h, wg_h, wv_h, ws_h) = refs[:11]
    (o_in, o_g, o_v, o_s) = refs[11:15]
    ev, ent, wg, wv, ws, in_sems = refs[15:21]
    it = iter(refs[21:])
    cumx, rowc, dyb, sdy, entb, gz, gxp, gxb, psum, acc, evt = [next(it) for _ in range(11)]
    tf, tsend, dsend, inc = [next(it) for _ in range(4)]
    crecv = [next(it) for _ in range(bits)]
    drecv = [next(it) for _ in range(bits)]
    csend = [next(it) for _ in range(bits - 1)]
    dnext = [next(it) for _ in range(bits - 1)]
    ifar = next(it)
    held = [[next(it) for _ in range(bits)] for _ in range(chunks)]
    land = [[next(it) for _ in range(bits)] for _ in range(chunks)]
    bcs, bcr, gis, gir = [next(it) for _ in range(4)]
    c_ss, c_rs, d_ss, d_rs, w_ss, w_rs, b_ss, b_rs, g_ss, g_rs = [next(it) for _ in range(10)]

    length, cols = x_in.shape
    state = b_in.shape[1]
    heads = ld_in.shape[0]
    width = cols // heads
    half = cols // 2
    rows = ev.shape[1] // n_ctx
    out_cols = ev.shape[1] // n_head
    pairs = cols // LANES
    per_pair = LANES // width

    me = lax.axis_index("ctx")
    hid = lax.axis_index("head")
    bit = [lax.rem(me // (1 << b), 2) for b in range(bits)]
    partner = [me + (1 - 2 * bit[b]) * (1 << b) for b in range(bits)]
    peers = [lax.rem(hid + r, n_head) for r in range(1, n_head)]
    core = bit[0]
    started = []
    fetch = [
        pltpu.make_async_copy(src, dst, in_sems.at[i])
        for i, (src, dst) in enumerate(
            ((ent_h, ent), (ev_h, ev), (wg_h, wg), (wv_h, wv), (ws_h, ws))
        )
    ]

    def send(src, dst, ss, rs, ctx_id, head_id):
        copy = pltpu.make_async_remote_copy(
            src_ref=src,
            dst_ref=dst,
            send_sem=ss,
            recv_sem=rs,
            device_id=(ctx_id, head_id),
            device_id_type=MESH,
        )
        copy.start()
        started.append(copy)
        return copy

    barrier = pltpu.get_barrier_semaphore()
    for p in partner:
        pl.semaphore_signal(barrier, inc=1, device_id=(p, hid), device_id_type=MESH)
    for p in peers:
        pl.semaphore_signal(barrier, inc=1, device_id=(me, p), device_id_type=MESH)

    for copy in fetch:
        copy.start()

    t_id = lax.broadcasted_iota(jnp.int32, (length, length), 0)
    s_id = lax.broadcasted_iota(jnp.int32, (length, length), 1)
    tril = t_id >= s_id
    triu = t_id <= s_id
    ld = ld_in[...]
    colcum = dot(tril.astype(F32), ld, (1, 1), HIGHEST)
    pick = (
        lax.broadcasted_iota(jnp.int32, (heads, cols), 1) // width
        == lax.broadcasted_iota(jnp.int32, (heads, cols), 0)
    ).astype(F32)
    cumx[...] = dot(colcum, pick, (1, 0), HIGHEST)
    rowc[...] = dot(ld, triu.astype(F32), (1, 0), HIGHEST)
    total = cumx[length - 1 : length, :]

    def at(k):
        return pl.ds(pl.multiple_of(k * LANES, LANES), LANES)

    def before(k, carry):
        sl = at(k)
        g = gate[:, sl].astype(F32)
        dy = gout[:, sl].astype(F32) * g * (1.0 / (1.0 + jnp.exp(-g)))
        dyb[:, sl] = dy.astype(BF16)
        sdy[:, sl] = (dy * jnp.exp(cumx[:, sl])).astype(BF16)
        return carry

    lax.fori_loop(0, pairs, before, 0)
    terms = dot(c_in[...], sdy[...], (0, 0))
    decays = jnp.broadcast_to(jnp.exp(total), (8, cols))
    for h in range(2):
        part = terms[:, h * half : (h + 1) * half]
        tf[h] = part
        tsend[h] = part.astype(BF16)
        dsend[h] = decays[:, h * half : (h + 1) * half]

    pl.semaphore_wait(barrier, bits + n_head - 1)

    flight = {}
    flight[0] = (
        send(tsend.at[1 - core], crecv[0], c_ss.at[0], c_rs.at[0], partner[0], hid),
        send(dsend.at[1 - core], drecv[0], d_ss.at[0], d_rs.at[0], partner[0], hid),
    )
    chain = {}

    def carry_step(k):
        if k == bits:
            flight[bits].wait_recv()
            return
        for copy in flight[k]:
            copy.wait_recv()
        other, other_d = crecv[k][...].astype(F32), drecv[k][0:1, :]
        early = bit[k] == 0
        if k == 0:
            mine, mine_d = tf[core], dsend[core][0:1, :]
            first = jnp.where(early, mine, other)
            last = jnp.where(early, other, mine)
            first_d = jnp.where(early, mine_d, other_d)
            last_d = jnp.where(early, other_d, mine_d)
            chain["last"], chain["last_d"] = last, last_d
            chain["t"] = first + first_d * last
            chain["d"] = first_d * last_d
            chain["x"] = jnp.zeros_like(last)
            chain["q"] = jnp.ones_like(last_d)
        else:
            t, d = chain["t"], chain["d"]
            chain["x"] = jnp.where(early, chain["x"] + chain["q"] * other, chain["x"])
            chain["q"] = jnp.where(early, chain["q"] * other_d, chain["q"])
            chain["t"] = jnp.where(early, t + d * other, other + other_d * t)
            chain["d"] = d * other_d
        if k < bits - 1:
            csend[k][...] = chain["t"].astype(BF16)
            dnext[k][...] = jnp.broadcast_to(chain["d"], (8, half))
            flight[k + 1] = (
                send(csend[k], crecv[k + 1], c_ss.at[k + 1], c_rs.at[k + 1], partner[k + 1], hid),
                send(dnext[k], drecv[k + 1], d_ss.at[k + 1], d_rs.at[k + 1], partner[k + 1], hid),
            )
        else:
            x = chain["x"]
            deeper = chain["last"] + chain["last_d"] * x
            ifar[...] = jnp.where(core == 0, x, deeper).astype(BF16)
            flight[bits] = send(
                ifar, inc.at[core], c_ss.at[bits], c_rs.at[bits], partner[0], hid
            )
            inc[core] = jnp.where(core == 0, deeper, x).astype(BF16)

    orders = split_orders(bits)
    rs_flight = {}

    def rs_send(c, k):
        order = orders[c % 2]
        b = order[k]
        count = n_ctx >> (k + 1)
        rs_flight[c, k] = send(
            held[c][k].at[pl.ds((1 - bit[b]) * count, count)],
            land[c][k],
            w_ss.at[c * bits + k],
            w_rs.at[c * bits + k],
            partner[b],
            hid,
        )

    def rs_begin(c, values):
        order = orders[c % 2]
        tile = min(256, ev.shape[1])
        for start in range(0, ev.shape[1], tile):
            part = dot(evt[start : start + tile, :], values).astype(BF16)
            for j in range(tile // rows):
                index = start // rows + j
                place = 0
                for k, b in enumerate(order):
                    place += ((index >> b) & 1) << (bits - 1 - k)
                held[c][0][place] = part[j * rows : (j + 1) * rows, :]
        rs_send(c, 0)

    outs = []

    def rs_step(c, k):
        order = orders[c % 2]
        b = order[k]
        count = n_ctx >> (k + 1)
        rs_flight[c, k].wait_recv()
        kept = held[c][k][pl.ds(bit[b] * count, count)].astype(F32) + land[c][k][...].astype(F32)
        if k < bits - 1:
            held[c][k + 1][...] = kept.astype(BF16)
            rs_send(c, k + 1)
        else:
            out, low, high = outs[c]
            out[:, low:high] = kept[0]

    per_kind = (chunks - 1) // 2
    step = cols // per_kind
    for out in (o_g, o_v):
        for j in range(per_kind):
            outs.append((out, j * step, (j + 1) * step))
    outs.append((o_s, 0, widths[-1]))

    scores = dot(c_in[...], b_in[...], (1, 1))
    scores_t = dot(b_in[...], c_in[...], (1, 1))
    fetch[0].wait()
    entb[...] = ent[...].astype(BF16)
    psum[...] = jnp.zeros_like(psum)
    lane = lax.broadcasted_iota(jnp.int32, (length, LANES), 1) // width

    def pair(k, carry):
        sl = at(k)
        x = x_in[:, sl]
        cum = cumx[:, sl]
        dyv = dyb[:, sl]
        dyf = dyv.astype(F32)
        y = jnp.exp(cum) * dot(c_in[...], entb[sl, :], (1, 1))
        gx = jnp.zeros((length, LANES), F32)
        both = psum[...]
        for q in range(per_pair):
            col = cum[:, q * width : q * width + 1]
            row = rowc[pl.ds(k * per_pair + q, 1), :]
            gap = col - row
            decay = jnp.where(tril, jnp.exp(jnp.minimum(gap, 0.0)), 0.0)
            decay_t = jnp.where(triu, jnp.exp(jnp.minimum(-gap, 0.0)), 0.0)
            own = lane == q
            y = y + jnp.where(own, dot((decay * scores).astype(BF16), x), 0.0)
            gx = gx + jnp.where(own, dot((decay_t * scores_t).astype(BF16), dyv), 0.0)
            both = both + decay * dot(jnp.where(own, dyf, 0.0).astype(BF16), x, (1, 1))
        psum[...] = both
        gxp[:, sl] = gx
        g = gate[:, sl].astype(F32)
        sig = 1.0 / (1.0 + jnp.exp(-g))
        gz[:, sl] = (gout[:, sl].astype(F32) * y * sig * (1.0 + g * (1.0 - sig))).astype(BF16)
        return carry

    group = pairs // per_kind
    gates = list(range(per_kind))
    values = list(range(per_kind, 2 * per_kind))
    last = chunks - 1
    reached = [0] * chunks

    def advance(which):
        for c in which:
            if reached[c] < bits:
                rs_step(c, reached[c])
                reached[c] += 1

    def some_pairs(i):
        lax.fori_loop(i * group, (i + 1) * group, pair, 0)

    def gate_begin(c):
        rs_begin(c, gz[:, c * step : (c + 1) * step])

    some_pairs(0)
    carry_step(0)
    fetch[1].wait()
    evt[...] = ev[...].T
    some_pairs(1)
    carry_step(1)
    gate_begin(0)
    for i in range(2, per_kind):
        some_pairs(i)
        gate_begin(i - 1)
        if i == 2:
            advance(gates[:1])
    carry_step(2)
    gate_begin(per_kind - 1)
    fetch[2].wait()
    acc[...] = dot(gz[...], wg[...], (1, 1))
    grad_c = dot(psum[...].astype(BF16), b_in[...]) + dot(sdy[...], entb[...])
    grad_b = dot(psum[...].T.astype(BF16), c_in[...])
    advance([c for c in gates[0::2] if reached[c] == 0])
    for k in range(3, bits):
        carry_step(k)
    advance(gates[1::2])
    carry_step(bits)

    def later_terms(c):
        cut = slice(c * step, (c + 1) * step)
        low = c * step % half
        into = inc[c * step // half][:, low : low + step]
        to_end = jnp.exp(total[:, cut] - cumx[:, cut])
        gxb[:, cut] = (gxp[:, cut] + to_end * dot(b_in[...], into)).astype(BF16)
        scaled = (x_in[:, cut].astype(F32) * to_end).astype(BF16)
        return dot(scaled, into, (1, 1))

    def value_begin(c):
        rs_begin(per_kind + c, gxb[:, c * step : (c + 1) * step])

    grad_b = grad_b + later_terms(0)
    value_begin(0)
    for c in range(1, per_kind):
        grad_b = grad_b + later_terms(c)
    bcs[:, 0:state] = grad_b.astype(BF16)
    bcs[:, state : 2 * state] = grad_c.astype(BF16)
    bc_copies = [
        send(bcs, bcr.at[r], b_ss.at[r], b_rs.at[r], me, p) for r, p in enumerate(peers)
    ]
    if per_kind > 1:
        value_begin(1)
    advance(gates[0::2])
    advance(values[0:2])
    for c in range(2, per_kind):
        value_begin(c)
    advance(gates[1::2])
    advance(values[2:])
    fetch[3].wait()
    acc[...] += dot(gxb[...], wv[...], (1, 1))
    advance(gates[0::2])
    grad_bc = jnp.concatenate([grad_b, grad_c], axis=1)
    for r, copy in enumerate(bc_copies):
        copy.wait_recv()
        grad_bc = grad_bc + bcr[r].astype(F32)
    sel = (
        lax.broadcasted_iota(jnp.int32, (2 * state, widths[-1]), 0)
        == lax.broadcasted_iota(jnp.int32, (2 * state, widths[-1]), 1) + hid * shared_cols
    ) & (lax.broadcasted_iota(jnp.int32, (2 * state, widths[-1]), 1) < shared_cols)
    shared = dot(grad_bc.astype(BF16), sel.astype(F32).astype(BF16)).astype(BF16)
    rs_begin(last, shared)
    fetch[4].wait()
    full = acc[...] + dot(shared, ws[...], (1, 1))
    for j in range(n_head):
        gis[j] = full[:, j * out_cols : (j + 1) * out_cols].astype(BF16)
    gi_copies = [
        send(gis.at[p], gir.at[r], g_ss.at[r], g_rs.at[r], me, p) for r, p in enumerate(peers)
    ]
    advance([last])
    while min(reached) < bits:
        advance(values)
        advance(gates)
        advance([last])
    grad_in = gis[hid].astype(F32)
    for r, copy in enumerate(gi_copies):
        copy.wait_recv()
        grad_in = grad_in + gir[r].astype(F32)
    o_in[...] = grad_in.astype(BF16)
    for copy in started:
        copy.wait_send()


def finish_kernel(scale, a, b, c, d, o_a, o_b, o_c, o_d):
    o_a[...] = a[...]
    o_b[...] = b[...] * scale
    o_c[...] = c[...] * scale
    o_d[...] = d[:, 0 : o_d.shape[1]] * scale


def per_device(
    n_ctx,
    n_head,
    events,
    ssm_input,
    gate_input,
    grad_out,
    shared_b,
    shared_c,
    log_decay,
    entry_state,
    w_gate,
    w_value,
    w_shared,
):
    length, cols = ssm_input.shape
    depth = events.shape[1]
    state = shared_b.shape[1]
    shared_cols = w_shared.shape[1]
    shared_wide = -(-shared_cols // LANES) * LANES
    if shared_wide > shared_cols:
        w_shared = jnp.pad(w_shared, ((0, 0), (0, shared_wide - shared_cols)))
    bits = n_ctx.bit_length() - 1
    rows = depth // n_ctx
    per_kind = max(1, min(4, cols // LANES))
    widths = [cols // per_kind] * (2 * per_kind) + [shared_wide]
    half = cols // 2
    entry = entry_state[0].transpose(0, 2, 1).reshape(cols, state)
    scale = 1.0 / math.sqrt(length * n_ctx)
    v = pltpu.VMEM
    dma = pltpu.SemaphoreType.DMA
    peers = n_head - 1
    scratch = [
        v(events.shape, BF16),
        v(entry.shape, F32),
        v(w_gate.shape, BF16),
        v(w_value.shape, BF16),
        v(w_shared.shape, BF16),
        dma((5,)),
        v((length, cols), F32),
        v((log_decay.shape[0], length), F32),
        v((length, cols), BF16),
        v((length, cols), BF16),
        v((cols, state), BF16),
        v((length, cols), BF16),
        v((length, cols), F32),
        v((length, cols), BF16),
        v((length, length), F32),
        v((length, depth), F32),
        v((depth, length), BF16),
        v((2, state, half), F32),
        v((2, state, half), BF16),
        v((2, 8, half), F32),
        v((2, state, half), BF16),
    ]
    scratch += [v((state, half), BF16) for _ in range(bits)]
    scratch += [v((8, half), F32) for _ in range(bits)]
    scratch += [v((state, half), BF16) for _ in range(bits - 1)]
    scratch += [v((8, half), F32) for _ in range(bits - 1)]
    scratch += [v((state, half), BF16)]
    for w in widths:
        scratch += [v((n_ctx >> k, rows, w), BF16) for k in range(bits)]
    for w in widths:
        scratch += [v((n_ctx >> (k + 1), rows, w), BF16) for k in range(bits)]
    scratch += [
        v((length, 2 * state), BF16),
        v((peers, length, 2 * state), BF16),
        v((n_head, length, depth // n_head), BF16),
        v((peers, length, depth // n_head), BF16),
        dma((bits + 1,)),
        dma((bits + 1,)),
        dma((bits,)),
        dma((bits,)),
        dma((len(widths) * bits,)),
        dma((len(widths) * bits,)),
        dma((peers,)),
        dma((peers,)),
        dma((peers,)),
        dma((peers,)),
    ]
    whole = pl.BlockSpec(memory_space=pltpu.VMEM)
    far = pl.BlockSpec(memory_space=pl.ANY)
    flops = 2 * length * (5 * state * cols + 3 * length * cols + 4 * depth * cols)
    results = pl.pallas_call(
        functools.partial(mixer_kernel, (n_ctx, n_head, widths, shared_cols)),
        out_shape=(
            jax.ShapeDtypeStruct((length, depth // n_head), BF16),
            jax.ShapeDtypeStruct((rows, cols), F32),
            jax.ShapeDtypeStruct((rows, cols), F32),
            jax.ShapeDtypeStruct((rows, shared_wide), F32),
        ),
        in_specs=[far, *[whole] * 6, far, far, far, far],
        out_specs=(whole,) * 4,
        scratch_shapes=scratch,
        compiler_params=pltpu.CompilerParams(
            collective_id=0, has_side_effects=True, vmem_limit_bytes=58 * 1024 * 1024
        ),
        cost_estimate=pl.CostEstimate(
            flops=flops, bytes_accessed=8 * 1024 * 1024, transcendentals=length * length * 32
        ),
        name="mixer",
    )(
        events,
        ssm_input,
        gate_input,
        grad_out,
        shared_b,
        shared_c,
        log_decay,
        entry,
        w_gate,
        w_value,
        w_shared,
    )
    return pl.pallas_call(
        functools.partial(finish_kernel, scale),
        out_shape=(
            *[jax.ShapeDtypeStruct(r.shape, r.dtype) for r in results[:3]],
            jax.ShapeDtypeStruct((rows, shared_cols), F32),
        ),
        in_specs=[whole] * 4,
        out_specs=(whole,) * 4,
        name="finish",
    )(*results)


def solution(mesh):
    placed = (
        P("ctx", None),
        P("ctx", "head"),
        P("ctx", "head"),
        P("ctx", "head"),
        P("ctx", None),
        P("ctx", None),
        P("head", "ctx"),
        P("ctx", "head", None, None),
        P(None, "head"),
        P(None, "head"),
        P(None, "head"),
    )
    return jax.shard_map(
        functools.partial(per_device, mesh.shape["ctx"], mesh.shape["head"]),
        mesh=mesh,
        in_specs=placed,
        out_specs=(P("ctx", "head"), P("ctx", "head"), P("ctx", "head"), P("ctx", "head")),
        check_vma=False,
    )
```

```python
import functools
import math

import jax
import jax.numpy as jnp
from jax import lax
from jax.experimental import pallas as pl
from jax.experimental.pallas import tpu as pltpu
from jax.sharding import PartitionSpec as P

F32 = jnp.float32
BF16 = jnp.bfloat16
HIGHEST = lax.Precision.HIGHEST
MESH = pl.DeviceIdType.MESH
LANES = 128


def dot(a, b, dims=(1, 0), precision=None):
    return lax.dot_general(
        a,
        b,
        (((dims[0],), (dims[1],)), ((), ())),
        preferred_element_type=F32,
        precision=precision,
    )


def split_orders(bits):
    plain = list(range(bits))
    swapped = list(plain)
    if bits >= 3:
        swapped[1], swapped[2] = swapped[2], swapped[1]
    return plain, swapped


def mixer_kernel(cfg, *refs):
    n_ctx, n_head, widths, shared_cols = cfg
    bits = n_ctx.bit_length() - 1
    chunks = len(widths)
    refs = list(refs)
    (ev_h, x_in, gate, gout, b_in, c_in, ld_in, ent_h, wg_h, wv_h, ws_h) = refs[:11]
    (o_in, o_g, o_v, o_s) = refs[11:15]
    ev, ent, wg, wv, ws, in_sems = refs[15:21]
    it = iter(refs[21:])
    cumx, rowc, dyb, sdy, entb, gz, gxp, gxb, psum, acc, evt = [next(it) for _ in range(11)]
    tf, tsend, dsend, inc = [next(it) for _ in range(4)]
    crecv = [next(it) for _ in range(bits)]
    drecv = [next(it) for _ in range(bits)]
    csend = [next(it) for _ in range(bits - 1)]
    dnext = [next(it) for _ in range(bits - 1)]
    ifar = next(it)
    held = [[next(it) for _ in range(bits)] for _ in range(chunks)]
    land = [[next(it) for _ in range(bits)] for _ in range(chunks)]
    bcs, bcr, gis, gir = [next(it) for _ in range(4)]
    c_ss, c_rs, d_ss, d_rs, w_ss, w_rs, b_ss, b_rs, g_ss, g_rs = [next(it) for _ in range(10)]

    length, cols = x_in.shape
    state = b_in.shape[1]
    heads = ld_in.shape[0]
    width = cols // heads
    half = cols // 2
    rows = ev.shape[1] // n_ctx
    out_cols = ev.shape[1] // n_head
    pairs = cols // LANES
    per_pair = LANES // width

    me = lax.axis_index("ctx")
    hid = lax.axis_index("head")
    bit = [lax.rem(me // (1 << b), 2) for b in range(bits)]
    partner = [me + (1 - 2 * bit[b]) * (1 << b) for b in range(bits)]
    peers = [lax.rem(hid + r, n_head) for r in range(1, n_head)]
    core = bit[0]
    started = []
    fetch = [
        pltpu.make_async_copy(src, dst, in_sems.at[i])
        for i, (src, dst) in enumerate(
            ((ent_h, ent), (ev_h, ev), (wg_h, wg), (wv_h, wv), (ws_h, ws))
        )
    ]

    def send(src, dst, ss, rs, ctx_id, head_id):
        copy = pltpu.make_async_remote_copy(
            src_ref=src,
            dst_ref=dst,
            send_sem=ss,
            recv_sem=rs,
            device_id=(ctx_id, head_id),
            device_id_type=MESH,
        )
        copy.start()
        started.append(copy)
        return copy

    barrier = pltpu.get_barrier_semaphore()
    for p in partner:
        pl.semaphore_signal(barrier, inc=1, device_id=(p, hid), device_id_type=MESH)
    for p in peers:
        pl.semaphore_signal(barrier, inc=1, device_id=(me, p), device_id_type=MESH)

    for copy in fetch:
        copy.start()

    t_id = lax.broadcasted_iota(jnp.int32, (length, length), 0)
    s_id = lax.broadcasted_iota(jnp.int32, (length, length), 1)
    tril = t_id >= s_id
    triu = t_id <= s_id
    ld = ld_in[...]
    colcum = dot(tril.astype(F32), ld, (1, 1), HIGHEST)
    pick = (
        lax.broadcasted_iota(jnp.int32, (heads, cols), 1) // width
        == lax.broadcasted_iota(jnp.int32, (heads, cols), 0)
    ).astype(F32)
    cumx[...] = dot(colcum, pick, (1, 0), HIGHEST)
    rowc[...] = dot(ld, triu.astype(F32), (1, 0), HIGHEST)
    total = cumx[length - 1 : length, :]

    def at(k):
        return pl.ds(pl.multiple_of(k * LANES, LANES), LANES)

    def before(k, carry):
        sl = at(k)
        g = gate[:, sl].astype(F32)
        dy = gout[:, sl].astype(F32) * g * (1.0 / (1.0 + jnp.exp(-g)))
        dyb[:, sl] = dy.astype(BF16)
        sdy[:, sl] = (dy * jnp.exp(cumx[:, sl])).astype(BF16)
        return carry

    lax.fori_loop(0, pairs, before, 0)
    terms = dot(c_in[...], sdy[...], (0, 0))
    decays = jnp.broadcast_to(jnp.exp(total), (8, cols))
    for h in range(2):
        part = terms[:, h * half : (h + 1) * half]
        tf[h] = part
        tsend[h] = part.astype(BF16)
        dsend[h] = decays[:, h * half : (h + 1) * half]

    pl.semaphore_wait(barrier, bits + n_head - 1)

    flight = {}
    flight[0] = (
        send(tsend.at[1 - core], crecv[0], c_ss.at[0], c_rs.at[0], partner[0], hid),
        send(dsend.at[1 - core], drecv[0], d_ss.at[0], d_rs.at[0], partner[0], hid),
    )
    chain = {}

    def carry_step(k):
        if k == bits:
            flight[bits].wait_recv()
            return
        for copy in flight[k]:
            copy.wait_recv()
        other, other_d = crecv[k][...].astype(F32), drecv[k][0:1, :]
        early = bit[k] == 0
        if k == 0:
            mine, mine_d = tf[core], dsend[core][0:1, :]
            first = jnp.where(early, mine, other)
            last = jnp.where(early, other, mine)
            first_d = jnp.where(early, mine_d, other_d)
            last_d = jnp.where(early, other_d, mine_d)
            chain["last"], chain["last_d"] = last, last_d
            chain["t"] = first + first_d * last
            chain["d"] = first_d * last_d
            chain["x"] = jnp.zeros_like(last)
            chain["q"] = jnp.ones_like(last_d)
        else:
            t, d = chain["t"], chain["d"]
            chain["x"] = jnp.where(early, chain["x"] + chain["q"] * other, chain["x"])
            chain["q"] = jnp.where(early, chain["q"] * other_d, chain["q"])
            chain["t"] = jnp.where(early, t + d * other, other + other_d * t)
            chain["d"] = d * other_d
        if k < bits - 1:
            csend[k][...] = chain["t"].astype(BF16)
            dnext[k][...] = jnp.broadcast_to(chain["d"], (8, half))
            flight[k + 1] = (
                send(csend[k], crecv[k + 1], c_ss.at[k + 1], c_rs.at[k + 1], partner[k + 1], hid),
                send(dnext[k], drecv[k + 1], d_ss.at[k + 1], d_rs.at[k + 1], partner[k + 1], hid),
            )
        else:
            x = chain["x"]
            deeper = chain["last"] + chain["last_d"] * x
            ifar[...] = jnp.where(core == 0, x, deeper).astype(BF16)
            flight[bits] = send(
                ifar, inc.at[core], c_ss.at[bits], c_rs.at[bits], partner[0], hid
            )
            inc[core] = jnp.where(core == 0, deeper, x).astype(BF16)

    orders = split_orders(bits)
    rs_flight = {}

    def rs_send(c, k):
        order = orders[c % 2]
        b = order[k]
        count = n_ctx >> (k + 1)
        rs_flight[c, k] = send(
            held[c][k].at[pl.ds((1 - bit[b]) * count, count)],
            land[c][k],
            w_ss.at[c * bits + k],
            w_rs.at[c * bits + k],
            partner[b],
            hid,
        )

    def rs_begin(c, values):
        order = orders[c % 2]
        tile = min(256, ev.shape[1])
        for start in range(0, ev.shape[1], tile):
            part = dot(evt[start : start + tile, :], values).astype(BF16)
            for j in range(tile // rows):
                index = start // rows + j
                place = 0
                for k, b in enumerate(order):
                    place += ((index >> b) & 1) << (bits - 1 - k)
                held[c][0][place] = part[j * rows : (j + 1) * rows, :]
        rs_send(c, 0)

    outs = []

    def rs_step(c, k):
        order = orders[c % 2]
        b = order[k]
        count = n_ctx >> (k + 1)
        rs_flight[c, k].wait_recv()
        kept = held[c][k][pl.ds(bit[b] * count, count)].astype(F32) + land[c][k][...].astype(F32)
        if k < bits - 1:
            held[c][k + 1][...] = kept.astype(BF16)
            rs_send(c, k + 1)
        else:
            out, low, high = outs[c]
            out[:, low:high] = kept[0]

    per_kind = (chunks - 1) // 2
    step = cols // per_kind
    for out in (o_g, o_v):
        for j in range(per_kind):
            outs.append((out, j * step, (j + 1) * step))
    outs.append((o_s, 0, widths[-1]))

    scores = dot(c_in[...], b_in[...], (1, 1))
    scores_t = dot(b_in[...], c_in[...], (1, 1))
    fetch[0].wait()
    entb[...] = ent[...].astype(BF16)
    psum[...] = jnp.zeros_like(psum)
    lane = lax.broadcasted_iota(jnp.int32, (length, LANES), 1) // width

    def pair(k, carry):
        sl = at(k)
        x = x_in[:, sl]
        cum = cumx[:, sl]
        dyv = dyb[:, sl]
        dyf = dyv.astype(F32)
        y = jnp.exp(cum) * dot(c_in[...], entb[sl, :], (1, 1))
        gx = jnp.zeros((length, LANES), F32)
        both = psum[...]
        for q in range(per_pair):
            col = cum[:, q * width : q * width + 1]
            row = rowc[pl.ds(k * per_pair + q, 1), :]
            gap = col - row
            decay = jnp.where(tril, jnp.exp(jnp.minimum(gap, 0.0)), 0.0)
            decay_t = jnp.where(triu, jnp.exp(jnp.minimum(-gap, 0.0)), 0.0)
            own = lane == q
            y = y + jnp.where(own, dot((decay * scores).astype(BF16), x), 0.0)
            gx = gx + jnp.where(own, dot((decay_t * scores_t).astype(BF16), dyv), 0.0)
            both = both + decay * dot(jnp.where(own, dyf, 0.0).astype(BF16), x, (1, 1))
        psum[...] = both
        gxp[:, sl] = gx
        g = gate[:, sl].astype(F32)
        sig = 1.0 / (1.0 + jnp.exp(-g))
        gz[:, sl] = (gout[:, sl].astype(F32) * y * sig * (1.0 + g * (1.0 - sig))).astype(BF16)
        return carry

    group = pairs // per_kind
    gates = list(range(per_kind))
    values = list(range(per_kind, 2 * per_kind))
    last = chunks - 1
    reached = [0] * chunks

    def advance(which):
        for c in which:
            if reached[c] < bits:
                rs_step(c, reached[c])
                reached[c] += 1

    def some_pairs(i):
        lax.fori_loop(i * group, (i + 1) * group, pair, 0)

    def gate_begin(c):
        rs_begin(c, gz[:, c * step : (c + 1) * step])

    some_pairs(0)
    carry_step(0)
    fetch[1].wait()
    evt[...] = ev[...].T
    some_pairs(1)
    carry_step(1)
    gate_begin(0)
    for i in range(2, per_kind):
        some_pairs(i)
        if i == 2:
            carry_step(2)
        gate_begin(i - 1)
    if per_kind <= 2:
        carry_step(2)
    gate_begin(per_kind - 1)
    grad_c = dot(psum[...].astype(BF16), b_in[...]) + dot(sdy[...], entb[...])
    grad_b = dot(psum[...].T.astype(BF16), c_in[...])
    advance(gates[0::2])
    for k in range(3, bits):
        carry_step(k)
    advance(gates[1::2])
    carry_step(bits)

    def later_terms(c):
        cut = slice(c * step, (c + 1) * step)
        low = c * step % half
        into = inc[c * step // half][:, low : low + step]
        to_end = jnp.exp(total[:, cut] - cumx[:, cut])
        gxb[:, cut] = (gxp[:, cut] + to_end * dot(b_in[...], into)).astype(BF16)
        scaled = (x_in[:, cut].astype(F32) * to_end).astype(BF16)
        return dot(scaled, into, (1, 1))

    def value_begin(c):
        rs_begin(per_kind + c, gxb[:, c * step : (c + 1) * step])

    grad_b = grad_b + later_terms(0)
    value_begin(0)
    for c in range(1, per_kind):
        grad_b = grad_b + later_terms(c)
    bcs[:, 0:state] = grad_b.astype(BF16)
    bcs[:, state : 2 * state] = grad_c.astype(BF16)
    bc_copies = [
        send(bcs, bcr.at[r], b_ss.at[r], b_rs.at[r], me, p) for r, p in enumerate(peers)
    ]
    if per_kind > 1:
        value_begin(1)
    advance(gates[0::2])
    advance(values[0:2])
    for c in range(2, per_kind):
        value_begin(c)
    advance(values[2:])
    advance(gates[1::2])
    fetch[2].wait()
    fetch[3].wait()
    acc[...] = dot(gz[...], wg[...], (1, 1)) + dot(gxb[...], wv[...], (1, 1))
    advance(gates[0::2])
    grad_bc = jnp.concatenate([grad_b, grad_c], axis=1)
    for r, copy in enumerate(bc_copies):
        copy.wait_recv()
        grad_bc = grad_bc + bcr[r].astype(F32)
    sel = (
        lax.broadcasted_iota(jnp.int32, (2 * state, widths[-1]), 0)
        == lax.broadcasted_iota(jnp.int32, (2 * state, widths[-1]), 1) + hid * shared_cols
    ) & (lax.broadcasted_iota(jnp.int32, (2 * state, widths[-1]), 1) < shared_cols)
    shared = dot(grad_bc.astype(BF16), sel.astype(F32).astype(BF16)).astype(BF16)
    rs_begin(last, shared)
    fetch[4].wait()
    full = acc[...] + dot(shared, ws[...], (1, 1))
    for j in range(n_head):
        gis[j] = full[:, j * out_cols : (j + 1) * out_cols].astype(BF16)
    gi_copies = [
        send(gis.at[p], gir.at[r], g_ss.at[r], g_rs.at[r], me, p) for r, p in enumerate(peers)
    ]
    advance([last])
    while min(reached) < bits:
        advance(values)
        advance(gates)
        advance([last])
    grad_in = gis[hid].astype(F32)
    for r, copy in enumerate(gi_copies):
        copy.wait_recv()
        grad_in = grad_in + gir[r].astype(F32)
    o_in[...] = grad_in.astype(BF16)
    for copy in started:
        copy.wait_send()


def finish_kernel(scale, a, b, c, d, o_a, o_b, o_c, o_d):
    o_a[...] = a[...]
    o_b[...] = b[...] * scale
    o_c[...] = c[...] * scale
    o_d[...] = d[:, 0 : o_d.shape[1]] * scale


def per_device(
    n_ctx,
    n_head,
    events,
    ssm_input,
    gate_input,
    grad_out,
    shared_b,
    shared_c,
    log_decay,
    entry_state,
    w_gate,
    w_value,
    w_shared,
):
    length, cols = ssm_input.shape
    depth = events.shape[1]
    state = shared_b.shape[1]
    shared_cols = w_shared.shape[1]
    shared_wide = -(-shared_cols // LANES) * LANES
    if shared_wide > shared_cols:
        w_shared = jnp.pad(w_shared, ((0, 0), (0, shared_wide - shared_cols)))
    bits = n_ctx.bit_length() - 1
    rows = depth // n_ctx
    per_kind = max(1, min(4, cols // LANES))
    widths = [cols // per_kind] * (2 * per_kind) + [shared_wide]
    half = cols // 2
    entry = entry_state[0].transpose(0, 2, 1).reshape(cols, state)
    scale = 1.0 / math.sqrt(length * n_ctx)
    v = pltpu.VMEM
    dma = pltpu.SemaphoreType.DMA
    peers = n_head - 1
    scratch = [
        v(events.shape, BF16),
        v(entry.shape, F32),
        v(w_gate.shape, BF16),
        v(w_value.shape, BF16),
        v(w_shared.shape, BF16),
        dma((5,)),
        v((length, cols), F32),
        v((log_decay.shape[0], length), F32),
        v((length, cols), BF16),
        v((length, cols), BF16),
        v((cols, state), BF16),
        v((length, cols), BF16),
        v((length, cols), F32),
        v((length, cols), BF16),
        v((length, length), F32),
        v((length, depth), F32),
        v((depth, length), BF16),
        v((2, state, half), F32),
        v((2, state, half), BF16),
        v((2, 8, half), F32),
        v((2, state, half), BF16),
    ]
    scratch += [v((state, half), BF16) for _ in range(bits)]
    scratch += [v((8, half), F32) for _ in range(bits)]
    scratch += [v((state, half), BF16) for _ in range(bits - 1)]
    scratch += [v((8, half), F32) for _ in range(bits - 1)]
    scratch += [v((state, half), BF16)]
    for w in widths:
        scratch += [v((n_ctx >> k, rows, w), BF16) for k in range(bits)]
    for w in widths:
        scratch += [v((n_ctx >> (k + 1), rows, w), BF16) for k in range(bits)]
    scratch += [
        v((length, 2 * state), BF16),
        v((peers, length, 2 * state), BF16),
        v((n_head, length, depth // n_head), BF16),
        v((peers, length, depth // n_head), BF16),
        dma((bits + 1,)),
        dma((bits + 1,)),
        dma((bits,)),
        dma((bits,)),
        dma((len(widths) * bits,)),
        dma((len(widths) * bits,)),
        dma((peers,)),
        dma((peers,)),
        dma((peers,)),
        dma((peers,)),
    ]
    whole = pl.BlockSpec(memory_space=pltpu.VMEM)
    far = pl.BlockSpec(memory_space=pl.ANY)
    flops = 2 * length * (5 * state * cols + 3 * length * cols + 4 * depth * cols)
    results = pl.pallas_call(
        functools.partial(mixer_kernel, (n_ctx, n_head, widths, shared_cols)),
        out_shape=(
            jax.ShapeDtypeStruct((length, depth // n_head), BF16),
            jax.ShapeDtypeStruct((rows, cols), F32),
            jax.ShapeDtypeStruct((rows, cols), F32),
            jax.ShapeDtypeStruct((rows, shared_wide), F32),
        ),
        in_specs=[far, *[whole] * 6, far, far, far, far],
        out_specs=(whole,) * 4,
        scratch_shapes=scratch,
        compiler_params=pltpu.CompilerParams(
            collective_id=0, has_side_effects=True, vmem_limit_bytes=58 * 1024 * 1024
        ),
        cost_estimate=pl.CostEstimate(
            flops=flops, bytes_accessed=8 * 1024 * 1024, transcendentals=length * length * 32
        ),
        name="mixer",
    )(
        events,
        ssm_input,
        gate_input,
        grad_out,
        shared_b,
        shared_c,
        log_decay,
        entry,
        w_gate,
        w_value,
        w_shared,
    )
    return pl.pallas_call(
        functools.partial(finish_kernel, scale),
        out_shape=(
            *[jax.ShapeDtypeStruct(r.shape, r.dtype) for r in results[:3]],
            jax.ShapeDtypeStruct((rows, shared_cols), F32),
        ),
        in_specs=[whole] * 4,
        out_specs=(whole,) * 4,
        name="finish",
    )(*results)


def solution(mesh):
    placed = (
        P("ctx", None),
        P("ctx", "head"),
        P("ctx", "head"),
        P("ctx", "head"),
        P("ctx", None),
        P("ctx", None),
        P("head", "ctx"),
        P("ctx", "head", None, None),
        P(None, "head"),
        P(None, "head"),
        P(None, "head"),
    )
    return jax.shard_map(
        functools.partial(per_device, mesh.shape["ctx"], mesh.shape["head"]),
        mesh=mesh,
        in_specs=placed,
        out_specs=(P("ctx", "head"), P("ctx", "head"), P("ctx", "head"), P("ctx", "head")),
        check_vma=False,
    )
```
